128 devices in a mesh: dp: 8 (over y, core), expert: 16 (over x, z).
Axes of the slice: x: 4, y: 4, z: 4, core: 2. Of those that a mesh axis runs over, the one named last changes fastest.
Arguments:
- tokens: bfloat16 [4096, 4096], P('expert', 'dp'), may hold values from -6 to 6
- expert_ids: int32 [4096, 8], P('expert'), may hold values from 0 to 63, all different within a row; in each aligned block of 256 rows (0 to 255, 256 to 511, ...) at most 48 rows name the same one
- route_weights: float32 [4096, 8], P('expert'), may hold values from 0.05 to 1
- w_gate: bfloat16 [64, 4096, 768], P('expert', 'dp'), may hold values from -0.09375 to 0.09375
- w_up: bfloat16 [64, 4096, 768], P('expert', 'dp'), may hold values from -0.09375 to 0.09375
- w_down: bfloat16 [64, 768, 4096], P('expert', None, 'dp'), may hold values from -0.21875 to 0.21875
- out_grad: bfloat16 [4096, 4096], P('expert', 'dp'), may hold values from -6 to 6
Outputs:
- mixed: bfloat16 [4096, 4096], P('expert', 'dp')
- grad_tokens: bfloat16 [4096, 4096], P('expert', 'dp')
- grad_route: float32 [4096, 8], P('expert')
- grad_gate: bfloat16 [64, 4096, 768], P('expert', 'dp')
- grad_up: bfloat16 [64, 4096, 768], P('expert', 'dp')
- grad_down: bfloat16 [64, 768, 4096], P('expert', None, 'dp')
The draws below stay inside these ranges and needn't reach their ends.
Inputs may be any that keep to these rules, and one draw needn't show every extreme that they name: `expert_ids`: each token names 8 different experts; within the 256 tokens of one index of the expert axis no expert is named more than 48 times, a bound that some block reaches.
All inputs are finite; a program needn't handle non-finite values.
Results may differ from the reference program's by a relative error of at most 0.033.
Values may be sent and summed in bfloat16 or wider, within the bound.
A program may use at most 128 MiB of HBM per device.

```python
import math
import jax
import jax.numpy as jnp
import numpy as np
from jax import lax

D = 4096
FF = 768
TOPK = 8
TOK = 256
EXPERTS = 64
CAP = 48
ROWS = 768
DS = 512
TOKENS = 4096
N_DP = 8
N_EXPERT = 16


def block_levels(own_key, dims, pieces, low, top_value):
    level = 1.0
    for position, blocks in pieces:
        heights = jax.random.uniform(jax.random.fold_in(jax.random.fold_in(own_key, 6), position), (blocks,), jnp.float32, low / len(pieces), top_value / len(pieces))
        level = level * jnp.repeat(jnp.exp(heights), dims[position] // blocks).reshape((-1,) + (1,) * (len(dims) - 1 - position))
    return level


def deal_out(key, own, number, rows, count, top, bound, skew):
    order = jax.random.permutation(key, count)
    heavy_load, common = load_shares(count, rows * top, bound, skew, True), load_shares(count, rows * top, bound, skew, False)
    places = jnp.arange(count)

    def named(lengths, turn):
        used = int((lengths > 0).sum())
        fixed = max(1, used // 4)
        shifted = fixed + (places - fixed + turn * (used - fixed)) % max(1, count - fixed)
        return jnp.zeros((count,), jnp.int32).at[order[jnp.where(places < fixed, places, shifted)]].set(jnp.asarray(lengths, jnp.int32))

    lengths = jnp.where(number % 4 == 0, named(heavy_load, number // 4), named(common, number - number // 4 - 1))
    mixed = jax.random.permutation(jax.random.fold_in(own, 3), count)
    source_of, sink = mixed[0:count // 2 * 2:2], mixed[1:count // 2 * 2:2]
    room = jnp.minimum(lengths[source_of] - 1, bound - lengths[sink]) // 2
    room = jnp.where((source_of == order[0]) | (sink == order[0]) | (lengths[sink] == 0), 0, jnp.maximum(room, 0))
    shifted = jax.random.randint(jax.random.fold_in(own, 4), (count // 2,), 0, 1 << 20) % (room + 1)
    lengths = lengths.at[source_of].add(-shifted).at[sink].add(shifted)
    members = jnp.searchsorted(jnp.cumsum(lengths), jnp.arange(rows * top), side="right").astype(jnp.int32)
    table = members.reshape(top, rows).T
    table = table[jax.random.permutation(jax.random.fold_in(own, 1), rows)]
    turn = jax.random.randint(jax.random.fold_in(own, 2), (rows, 1), 0, top)
    return jnp.take_along_axis(table, (jnp.arange(top)[None, :] + turn) % top, axis=1)


def load_shares(number_of, total, limit, lean, full):
    portions = [(1 << 20) // math.isqrt(grade ** lean) + 1 for grade in range(1, number_of + 1)]
    largest = limit if full else min(limit, max(-(-total // number_of), total * portions[0] // sum(portions)))
    least = 1 if total - largest >= number_of - 1 else 0
    given, surplus = [largest] + [least] * (number_of - 1), total - largest - least * (number_of - 1)
    while surplus > 0:
        candidates = [i for i in range(1, number_of) if given[i] < largest] or [i for i in range(1, number_of) if given[i] < limit]
        whole, remaining = sum([portions[i] for i in candidates]), surplus
        for i in candidates:
            more = min(limit - given[i], max(1, remaining * portions[i] // whole), surplus)
            given[i] = given[i] + more
            surplus = surplus - more
    return np.array(given)


def gaussian(key, dims, spread, bound, cuts=(), kind=jnp.bfloat16):
    result = spread * jax.random.normal(key, dims, jnp.float32)
    if cuts:
        result = result * block_levels(key, dims, cuts, -0.22, 0.18)
    return jnp.clip(result, -bound, bound).astype(kind)


def setup_inputs(seed: int = 0) -> dict:
    key_list = jax.random.split(jax.random.key(seed), 8)
    tokens = gaussian(key_list[0], (TOKENS, D), 1.0, 6.0, ((0, 16), (1, 8)))
    expert_ids_keys = jax.random.split(jax.random.fold_in(key_list[1], 1), TOKENS // TOK)
    expert_ids_turns = jax.random.permutation(jax.random.fold_in(key_list[1], 3), TOKENS // TOK)
    expert_ids = jax.vmap(lambda own, number: deal_out(jax.random.fold_in(key_list[1], 2), own, number, TOK, EXPERTS, TOPK, CAP, 2))(expert_ids_keys, expert_ids_turns).reshape((TOKENS, TOPK))
    route_weights = jnp.clip(jnp.exp(math.log(1.0) - 2.9957323 * jax.random.uniform(key_list[2], (TOKENS, TOPK), jnp.float32) ** block_levels(key_list[2], (TOKENS, TOPK), ((0, 16),), -0.2, 0.2)), 0.05, 1.0)
    w_gate = gaussian(key_list[3], (EXPERTS, D, FF), D ** -0.5, 0.09375, ((0, 16), (1, 8)))
    w_up = gaussian(key_list[4], (EXPERTS, D, FF), D ** -0.5, 0.09375, ((0, 16), (1, 8)))
    w_down = gaussian(key_list[5], (EXPERTS, FF, D), FF ** -0.5, 0.21875, ((0, 16), (2, 8)))
    out_grad = gaussian(key_list[6], (TOKENS, D), 1.0, 6.0, ((0, 16), (1, 8)))
    return {"tokens": tokens, "expert_ids": expert_ids, "route_weights": route_weights, "w_gate": w_gate, "w_up": w_up, "w_down": w_down, "out_grad": out_grad}


def grouped(left, weight):
    width = weight.shape[1]
    parts = jnp.einsum("rgd,gdf->grf", left.reshape(ROWS, N_DP, DS).astype(jnp.float32), weight.reshape(N_DP, DS, width).astype(jnp.float32))
    rounded = lax.optimization_barrier(parts.astype(jnp.bfloat16))
    return jnp.sum(rounded.astype(jnp.float32), 0)


def reference(tokens, expert_ids, route_weights, w_gate, w_up, w_down, out_grad):
    blocks = expert_ids.reshape(N_EXPERT, TOK, TOPK)
    table = jnp.arange(EXPERTS, dtype=jnp.int32)
    member = (blocks[..., None] == table).astype(jnp.int32)
    counts = jnp.sum(member, 2)
    before = jnp.cumsum(counts, 1) - counts
    rank = jnp.sum(member * before[:, :, None, :], 3).reshape(TOKENS, TOPK)
    source = (jnp.arange(TOKENS, dtype=jnp.int32) // TOK).astype(jnp.int32)
    grad_f = out_grad.astype(jnp.float32)
    zero_row = jnp.zeros((1, D), jnp.bfloat16)

    def step(carry, xs):
        mixed_acc, grad_acc, route_acc = carry
        wg, wu, wd, expert = xs
        hitk = expert_ids == expert
        hit = jnp.any(hitk, 1)
        rank_e = jnp.sum(jnp.where(hitk, rank, 0), 1).astype(jnp.int32)
        weight_e = jnp.sum(jnp.where(hitk, route_weights, 0.0), 1)
        index = jnp.where(hit, source * CAP + rank_e, ROWS).astype(jnp.int32)
        expert_in = jnp.zeros((ROWS + 1, D), jnp.bfloat16).at[index].set(tokens)[:ROWS]
        scaled = (weight_e[:, None] * grad_f).astype(jnp.bfloat16)
        slot_grad_in = jnp.zeros((ROWS + 1, D), jnp.bfloat16).at[index].set(scaled)[:ROWS]
        gate = grouped(expert_in, wg)
        up = grouped(expert_in, wu)
        hidden = (jax.nn.silu(gate) * up).astype(jnp.bfloat16)
        expert_out = jnp.dot(hidden, wd, preferred_element_type=jnp.float32).astype(jnp.bfloat16)
        picked = jnp.concatenate([expert_out, zero_row], 0)[index]
        mixed_acc = mixed_acc + weight_e[:, None] * picked.astype(jnp.float32)
        parts = jnp.sum((grad_f * picked.astype(jnp.float32)).reshape(TOKENS, N_DP, DS), 2)
        parts = lax.optimization_barrier(parts.astype(jnp.bfloat16))
        route_e = jnp.sum(parts.astype(jnp.float32), 1)
        route_acc = route_acc + jnp.where(hitk, route_e[:, None], 0.0)
        grad_down = jnp.dot(hidden.T, slot_grad_in, preferred_element_type=jnp.float32).astype(jnp.bfloat16)
        grad_hidden = grouped(slot_grad_in, wd.T)
        sig = jax.nn.sigmoid(gate)
        d_gate = (grad_hidden * up * sig * (1.0 + gate * (1.0 - sig))).astype(jnp.bfloat16)
        d_up = (grad_hidden * jax.nn.silu(gate)).astype(jnp.bfloat16)
        grad_gate = jnp.dot(expert_in.T, d_gate, preferred_element_type=jnp.float32).astype(jnp.bfloat16)
        grad_up = jnp.dot(expert_in.T, d_up, preferred_element_type=jnp.float32).astype(jnp.bfloat16)
        slot_grad_out = (jnp.dot(d_gate, wg.T, preferred_element_type=jnp.float32) + jnp.dot(d_up, wu.T, preferred_element_type=jnp.float32)).astype(jnp.bfloat16)
        back = jnp.concatenate([slot_grad_out, zero_row], 0)[index]
        grad_acc = grad_acc + back.astype(jnp.float32)
        return (mixed_acc, grad_acc, route_acc), (grad_gate, grad_up, grad_down)

    start = (jnp.zeros((TOKENS, D), jnp.float32), jnp.zeros((TOKENS, D), jnp.float32), jnp.zeros((TOKENS, TOPK), jnp.float32))
    carry, stacked = lax.scan(step, start, (w_gate, w_up, w_down, jnp.arange(EXPERTS, dtype=jnp.int32)))
    mixed_acc, grad_acc, route_acc = carry
    grad_gate, grad_up, grad_down = stacked
    return (mixed_acc.astype(jnp.bfloat16), grad_acc.astype(jnp.bfloat16), route_acc, grad_gate, grad_up, grad_down)
```

```python
import jax
import jax.numpy as jnp
from jax import lax
from jax.sharding import PartitionSpec as P

F32 = jnp.float32
BF16 = jnp.bfloat16


def local(tokens, expert_ids, route_weights, w_gate, w_up, w_down, out_grad):
    tok, top = expert_ids.shape
    e_loc, width, ff = w_gate.shape
    owners = lax.axis_size("expert")
    n_dp = lax.axis_size("dp")
    experts = e_loc * owners
    cap = 3 * tok * top // (2 * experts)
    rows = owners * cap
    table = jnp.arange(experts, dtype=jnp.int32)
    hit = expert_ids[:, None, :] == table[None, :, None]
    member = jnp.any(hit, 2)
    tri = (jnp.arange(tok)[:, None] > jnp.arange(tok)[None, :]).astype(BF16)
    before = jnp.dot(tri, member.astype(BF16), preferred_element_type=F32).astype(jnp.int32)
    rank = jnp.where(member, before, -1)
    weight = jnp.sum(jnp.where(hit, route_weights[:, None, :], 0.0), 2).astype(BF16)
    pick = rank.T[:, None, :] == jnp.arange(cap, dtype=jnp.int32)[None, :, None]
    one = pick.astype(BF16).reshape(experts * cap, tok)
    scaled = jnp.where(pick, weight.T[:, None, :], 0).astype(BF16).reshape(experts * cap, tok)
    layout = (owners, e_loc, cap, width)

    def out(v):
        return lax.all_to_all(v.reshape(layout), "expert", split_axis=0, concat_axis=2, tiled=True)[0]

    x = out(jnp.dot(one, tokens, preferred_element_type=F32).astype(BF16))
    g = out(jnp.dot(scaled, out_grad, preferred_element_type=F32).astype(BF16))
    part = jnp.concatenate(
        (
            jnp.einsum("erd,edf->erf", x, w_gate, preferred_element_type=F32).astype(BF16),
            jnp.einsum("erd,edf->erf", x, w_up, preferred_element_type=F32).astype(BF16),
            jnp.einsum("erd,efd->erf", g, w_down, preferred_element_type=F32).astype(BF16),
        ),
        -1,
    )
    full = lax.psum_scatter(part, "dp", scatter_dimension=1, tiled=True).astype(F32)
    gate, up, gh = full[..., :ff], full[..., ff : 2 * ff], full[..., 2 * ff :]
    sig = jax.nn.sigmoid(gate)
    act = gate * sig
    hid = (act * up).astype(BF16)
    dg = (gh * up * sig * (1.0 + gate * (1.0 - sig))).astype(BF16)
    du = (gh * act).astype(BF16)
    route = jnp.sum(hid.astype(F32) * gh, -1)
    every = lax.all_gather(jnp.concatenate((hid, dg, du), -1), "dp", axis=1, tiled=True)
    hid, dg, du = every[..., :ff], every[..., ff : 2 * ff], every[..., 2 * ff :]
    eo = jnp.einsum("erf,efd->erd", hid, w_down, preferred_element_type=F32).astype(BF16)
    so = (
        jnp.einsum("erf,edf->erd", dg, w_gate, preferred_element_type=F32)
        + jnp.einsum("erf,edf->erd", du, w_up, preferred_element_type=F32)
    ).astype(BF16)

    def back(v):
        v = lax.all_to_all(v, "expert", split_axis=1, concat_axis=0, tiled=True)
        return v.reshape(experts * cap, -1)

    mixed = jnp.einsum("st,sd->td", scaled, back(eo), preferred_element_type=F32).astype(BF16)
    grad_tokens = jnp.einsum("st,sd->td", one, back(so), preferred_element_type=F32).astype(BF16)
    grad_down = jnp.einsum("erf,erd->efd", hid, g, preferred_element_type=F32).astype(BF16)
    grad_gate = jnp.einsum("erd,erf->edf", x, dg, preferred_element_type=F32).astype(BF16)
    grad_up = jnp.einsum("erd,erf->edf", x, du, preferred_element_type=F32).astype(BF16)
    route = lax.all_gather(lax.all_gather(route, "dp", axis=1, tiled=True), "expert", axis=0, tiled=True)
    mine = lax.dynamic_slice_in_dim(route, lax.axis_index("expert") * cap, cap, 1)
    per = jnp.sum(jnp.where(pick, mine[:, :, None], 0.0), 1)
    grad_route = jnp.sum(jnp.where(hit, per.T[:, :, None], 0.0), 1)
    grad_route = grad_route / route_weights.astype(BF16).astype(F32)
    return (mixed, grad_tokens, grad_route, grad_gate, grad_up, grad_down)


def solution(mesh):
    tok = P("expert", "dp")
    whole = P("expert", None)
    wide = P("expert", "dp", None)
    down = P("expert", None, "dp")
    return jax.shard_map(
        local,
        mesh=mesh,
        in_specs=(tok, whole, whole, wide, wide, down, tok),
        out_specs=(tok, tok, whole, wide, wide, down),
        check_vma=False,
    )
```

```python
import jax
import jax.numpy as jnp
from jax import lax
from jax.experimental import pallas as pl
from jax.experimental.pallas import tpu as pltpu
from jax.sharding import PartitionSpec as P

F32 = jnp.float32
BF16 = jnp.bfloat16
MESH = pl.DeviceIdType.MESH
NN = ((1,), (0,))
NT = ((1,), (1,))
TN = ((0,), (0,))


def dot(a, b, dims):
    return lax.dot_general(a, b, (dims, ((), ())), preferred_element_type=F32)


def kernel(
    rank_ref, weight_ref, tok_ref, og_ref, wg_hbm, wu_hbm, wd_hbm,
    mixed_ref, gtok_ref, route_ref, gg_hbm, gu_hbm, gd_hbm,
    wg, wu, wd, one, scaled, sent, xg, mine, held, far, act, back, st_g, st_u, st_d,
    acc_m, acc_t, dr_all, dr_in,
    w_sem, o_sem, d_send, d_recv, h_send, h_recv, r_send, r_recv, a_send, a_recv, c_send, c_recv,
    t_send, t_recv, q_send, q_recv, v_send, v_recv,
):
    n_e, _, rows, _ = sent.shape
    ff = wg.shape[2]
    n_o = lax.axis_size("expert")
    n_dp = lax.axis_size("dp")
    n_y = n_dp // 2
    cap = rows // n_o
    half = rows // 2
    part = half // n_y
    dp = lax.axis_index("dp")
    me = lax.axis_index("expert")
    y, core = dp // 2, dp % 2
    share = core * n_y + y
    own0 = pl.multiple_of(core * half, half)
    other0 = pl.multiple_of((1 - core) * half, half)
    part0 = pl.multiple_of(own0 + y * part, part)

    def remote(src, dst, ss, rs, d, o):
        return pltpu.make_async_remote_copy(
            src_ref=src, dst_ref=dst, send_sem=ss, recv_sem=rs, device_id=(d, o), device_id_type=MESH
        )

    def block(o):
        return pl.ds(pl.multiple_of(o * cap, cap), cap)

    def drain(ref, sem):
        pltpu.make_async_copy(ref, ref, sem).wait()

    loads = [pltpu.make_async_copy(h, v, w_sem.at[i]) for i, (h, v) in enumerate(((wg_hbm, wg), (wu_hbm, wu), (wd_hbm, wd)))]
    for c in loads:
        c.start()

    barrier = pltpu.get_barrier_semaphore()

    @pl.loop(1, n_o)
    def _(k):
        pl.semaphore_signal(barrier, inc=1, device_id=(dp, lax.rem(me + k, n_o)), device_id_type=MESH)

    @pl.loop(1, n_dp)
    def _(k):
        pl.semaphore_signal(barrier, inc=1, device_id=(lax.rem(dp + k, n_dp), me), device_id_type=MESH)

    def build(e):
        @pl.loop(0, n_o)
        def _(o):
            i = e * n_o + o
            r = rank_ref[pl.ds(i, 1), :]
            w = weight_ref[pl.ds(i, 1), :]
            m = r == lax.broadcasted_iota(jnp.int32, (cap, r.shape[1]), 0)
            at = pl.ds(pl.multiple_of(i * cap, cap), cap)
            one[at, :] = jnp.where(m, 1.0, 0.0).astype(BF16)
            scaled[at, :] = jnp.where(m, w, 0.0).astype(BF16)

        for half_, (mat, src) in enumerate(((one, tok_ref), (scaled, og_ref))):
            @pl.loop(0, rows // 256)
            def _(i, half_=half_, mat=mat, src=src):
                r0 = pl.multiple_of(i * 256, 256)
                sent[e, half_, pl.ds(r0, 256), :] = dot(mat[pl.ds(e * rows + r0, 256), :], src[...], NN).astype(BF16)

    def spread(src, dst, ss, rs, e):
        for h in range(2):
            @pl.loop(1, n_o)
            def _(k, h=h):
                to = lax.rem(me + k, n_o)
                remote(src.at[e, h, block(to)], dst.at[e, h, block(me)], ss.at[e, h], rs.at[e, h], dp, to).start()
            pltpu.make_async_copy(src.at[e, h, block(me)], dst.at[e, h, block(me)], rs.at[e, h]).start()

    def sent_all(e, ss):
        for h in range(2):
            drain(sent.at[e, h, pl.ds(0, rows - cap)], ss.at[e, h])

    def product(e, r0, store):
        @pl.loop(0, half // 192)
        def _(i):
            at = pl.ds(pl.multiple_of(r0 + i * 192, 192), 192)
            to = pl.ds(pl.multiple_of(i * 192, 192), 192)
            x = xg[e, 0, at, :]
            g = xg[e, 1, at, :]
            store[to, 0:ff] = dot(x, wg[e], NN).astype(BF16)
            store[to, ff : 2 * ff] = dot(x, wu[e], NN).astype(BF16)
            store[to, 2 * ff : 3 * ff] = dot(g, wd[e], NT).astype(BF16)

    def stage_d(e):
        for h in range(2):
            drain(xg.at[e, h], d_recv.at[e, h])
        if e == 0:
            for c in loads:
                c.wait()
        product(e, other0, mine.at[2])
        remote(mine.at[2], held.at[e % 2], h_send.at[e], h_recv.at[e], y * 2 + 1 - core, me).start()
        product(e, own0, mine.at[e % 2])

    def stage_r(e):
        cp = remote(mine.at[2], held.at[e % 2], h_send.at[e], h_recv.at[e], y * 2 + 1 - core, me)
        cp.wait_recv()
        for d in (2, 1, 3, 0):
            to = lax.rem(y + d, n_y)
            at = pl.ds(pl.multiple_of(to * part, part), part)
            own = mine.at[e % 2, at]
            own[...] = (own[...].astype(F32) + held[e % 2, at, :].astype(F32)).astype(BF16)
            if d:
                remote(own, far.at[e, d - 1], r_send.at[e, d - 1], r_recv.at[e, d - 1], to * 2 + core, me).start()
        cp.wait_send()

    def stage_a(e):
        for d in (1, 2, 3):
            drain(far.at[e, d - 1], r_recv.at[e, d - 1])
        at = pl.ds(pl.multiple_of(y * part, part), part)

        def total(c0):
            v = mine[e % 2, at, c0 : c0 + ff].astype(F32)
            for d in range(3):
                v = v + far[e, d, :, c0 : c0 + ff].astype(F32)
            return v

        gate, up, gh = total(0), total(ff), total(2 * ff)
        sig = 1.0 / (1.0 + jnp.exp(-gate))
        silu = gate * sig
        hid = (silu * up).astype(BF16)
        out = act.at[e % 3, pl.ds(part0, part)]
        out[:, 0:ff] = hid
        out[:, ff : 2 * ff] = (gh * up * sig * (1.0 + gate * (1.0 - sig))).astype(BF16)
        out[:, 2 * ff : 3 * ff] = (gh * silu).astype(BF16)
        for d in (2, 1, 3):
            remote(out, out, a_send.at[e, d - 1], a_recv.at[e, d - 1], lax.rem(y + d, n_y) * 2 + core, me).start()
        prod = (hid.astype(F32) * gh).astype(BF16)
        row = dot(jnp.ones((8, ff), BF16), prod, NT)
        dr_all[share, e : e + 1, 0:part] = row[0:1]
        for d in (1, 2, 3):
            drain(far.at[e, d - 1], r_send.at[e, d - 1])

    def stage_f(e):
        own = act.at[e % 3, pl.ds(part0, part)]
        for d in (1, 2, 3):
            drain(own, a_recv.at[e, d - 1])
            drain(own, a_send.at[e, d - 1])
        mine_ = act.at[e % 3, pl.ds(own0, half)]
        remote(mine_, mine_, c_send.at[e], c_recv.at[e], y * 2 + 1 - core, me).start()

    def stage_c(e):
        mine_ = act.at[e % 3, pl.ds(own0, half)]
        remote(mine_, mine_, c_send.at[e], c_recv.at[e], y * 2 + 1 - core, me).wait()
        sent_all(e, d_send)

        @pl.loop(0, rows // 256)
        def _(i):
            at = pl.ds(pl.multiple_of(i * 256, 256), 256)
            sent[e, 0, at, :] = dot(act[e % 3, at, 0:ff], wd[e], NN).astype(BF16)
            so = dot(act[e % 3, at, ff : 2 * ff], wg[e], NT) + dot(act[e % 3, at, 2 * ff : 3 * ff], wu[e], NT)
            sent[e, 1, at, :] = so.astype(BF16)

        spread(sent, back, t_send, t_recv, e)
        if e:
            for c in stored(e - 1):
                c.wait()

        @pl.loop(0, ff // 256)
        def _(i):
            at = pl.ds(pl.multiple_of(i * 256, 256), 256)
            st_d[at, :] = dot(act[e % 3, :, at], xg[e, 1], TN).astype(BF16)

        @pl.loop(0, xg.shape[3] // 256)
        def _(i):
            at = pl.ds(pl.multiple_of(i * 256, 256), 256)
            x = xg[e, 0, :, at]
            st_g[at, :] = dot(x, act[e % 3, :, ff : 2 * ff], TN).astype(BF16)
            st_u[at, :] = dot(x, act[e % 3, :, 2 * ff : 3 * ff], TN).astype(BF16)

        for c in stored(e):
            c.start()

    def stored(e):
        return (
            pltpu.make_async_copy(st_g, gg_hbm.at[e], o_sem.at[0]),
            pltpu.make_async_copy(st_u, gu_hbm.at[e], o_sem.at[1]),
            pltpu.make_async_copy(st_d, gd_hbm.at[e], o_sem.at[2]),
        )

    def gather(e):
        at = pl.ds(e * rows, rows)
        for h, (mat, acc) in enumerate(((scaled, acc_m), (one, acc_t))):
            drain(back.at[e, h], t_recv.at[e, h])
            v = dot(mat[at, :], back[e, h], TN)
            if e == 0:
                acc[...] = v
            else:
                acc[...] += v

    dr_all[share] = jnp.zeros(dr_all.shape[1:], F32)
    build(0)
    pl.semaphore_wait(barrier, n_o + n_dp - 2)
    spread(sent, xg, d_send, d_recv, 0)
    for e in range(1, n_e):
        build(e)
        spread(sent, xg, d_send, d_recv, e)
    stage_d(0)
    stage_r(0)
    stage_d(1)
    stage_r(1)
    stage_a(0)
    stage_d(2)
    stage_r(2)
    stage_a(1)
    stage_f(0)
    stage_c(0)
    stage_d(3)
    stage_r(3)
    stage_a(2)
    stage_f(1)
    stage_c(1)
    stage_a(3)

    @pl.loop(1, n_dp)
    def _(k):
        own = dr_all.at[share]
        remote(own, own, q_send, q_recv, lax.rem(dp + k, n_dp), me).start()

    stage_f(2)
    stage_c(2)
    stage_f(3)
    drain(dr_all.at[pl.ds(0, n_dp - 1)], q_recv)
    drain(dr_all.at[pl.ds(0, n_dp - 1)], q_send)

    @pl.loop(1, n_o)
    def _(k):
        to = lax.rem(me + k, n_o)
        remote(dr_all.at[to // 2], dr_in.at[me], v_send, v_recv, dp, to).start()

    pltpu.make_async_copy(dr_all.at[me // 2], dr_in.at[me], v_recv).start()
    stage_c(3)
    gather(0)
    gather(1)
    gather(2)
    drain(dr_in, v_recv)
    drain(dr_in.at[pl.ds(0, n_o - 1)], v_send)
    route_ref[...] = dr_in[...]
    gather(3)
    mixed_ref[...] = acc_m[...].astype(BF16)
    gtok_ref[...] = acc_t[...].astype(BF16)
    for e in range(n_e):
        sent_all(e, t_send)
    for c in stored(n_e - 1):
        c.wait()


def local(tokens, expert_ids, route_weights, w_gate, w_up, w_down, out_grad):
    tok, top = expert_ids.shape
    e_loc, width, ff = w_gate.shape
    owners = lax.axis_size("expert")
    n_dp = lax.axis_size("dp")
    experts = e_loc * owners
    cap = 3 * tok * top // (2 * experts)
    rows = owners * cap
    half, part = rows // 2, rows // n_dp
    table = jnp.arange(experts, dtype=jnp.int32)
    hit = expert_ids[:, :, None] == table
    member = jnp.any(hit, 1)
    tri = (jnp.arange(tok)[:, None] > jnp.arange(tok)[None, :]).astype(BF16)
    before = jnp.dot(tri, member.astype(BF16), preferred_element_type=F32).astype(jnp.int32)
    rank = jnp.where(member, before, -1)
    rounded = route_weights.astype(BF16).astype(F32)
    weight = jnp.sum(jnp.where(hit, rounded[:, :, None], 0.0), 1)

    def order(v):
        return v.T.reshape(owners, e_loc, tok).transpose(1, 0, 2).reshape(experts, tok)

    rank, weight = order(rank), order(weight)
    vm = pl.BlockSpec(memory_space=pltpu.VMEM)
    hbm = pl.BlockSpec(memory_space=pl.ANY)
    dma = pltpu.SemaphoreType.DMA
    mixed, gtok, route, gg, gu, gd = pl.pallas_call(
        kernel,
        out_shape=(
            jax.ShapeDtypeStruct((tok, width), BF16),
            jax.ShapeDtypeStruct((tok, width), BF16),
            jax.ShapeDtypeStruct((owners, 8, 128), F32),
            jax.ShapeDtypeStruct((e_loc, width, ff), BF16),
            jax.ShapeDtypeStruct((e_loc, width, ff), BF16),
            jax.ShapeDtypeStruct((e_loc, ff, width), BF16),
        ),
        in_specs=[vm] * 4 + [hbm] * 3,
        out_specs=[vm] * 3 + [hbm] * 3,
        scratch_shapes=[
            pltpu.VMEM((e_loc, width, ff), BF16),
            pltpu.VMEM((e_loc, width, ff), BF16),
            pltpu.VMEM((e_loc, ff, width), BF16),
            pltpu.VMEM((e_loc * rows, tok), BF16),
            pltpu.VMEM((e_loc * rows, tok), BF16),
            pltpu.VMEM((e_loc, 2, rows, width), BF16),
            pltpu.VMEM((e_loc, 2, rows, width), BF16),
            pltpu.VMEM((3, half, 3 * ff), BF16),
            pltpu.VMEM((2, half, 3 * ff), BF16),
            pltpu.VMEM((e_loc, 3, part, 3 * ff), BF16),
            pltpu.VMEM((3, rows, 3 * ff), BF16),
            pltpu.VMEM((e_loc, 2, rows, width), BF16),
            pltpu.VMEM((width, ff), BF16),
            pltpu.VMEM((width, ff), BF16),
            pltpu.VMEM((ff, width), BF16),
            pltpu.VMEM((tok, width), F32),
            pltpu.VMEM((tok, width), F32),
            pltpu.VMEM((n_dp, 8, 128), F32),
            pltpu.VMEM((owners, 8, 128), F32),
            dma((3,)), dma((3,)), dma((4, 2)), dma((4, 2)), dma((4,)), dma((4,)),
            dma((4, 3)), dma((4, 3)), dma((4, 3)), dma((4, 3)), dma((4,)), dma((4,)),
            dma((4, 2)), dma((4, 2)), dma, dma, dma, dma,
        ],
        compiler_params=pltpu.CompilerParams(
            collective_id=0, has_side_effects=True, vmem_limit_bytes=61 * 2**20
        ),
        name="moe",
    )(rank, weight, tokens, out_grad, w_gate, w_up, w_down)
    at = (lax.axis_index("expert") % 2) * cap
    per = lax.dynamic_slice_in_dim(route[:, :e_loc], at, cap, 2)
    per = per.transpose(1, 0, 2).reshape(experts, cap)
    pick = rank[:, None, :] == jnp.arange(cap, dtype=jnp.int32)[None, :, None]
    value = jnp.sum(jnp.where(pick, per[:, :, None], 0.0), 1)
    value = value.reshape(e_loc, owners, tok).transpose(1, 0, 2).reshape(experts, tok)
    grad_route = jnp.sum(jnp.where(hit, value.T[:, None, :], 0.0), 2) / rounded
    return (mixed, gtok, grad_route, gg, gu, gd)


def solution(mesh):
    tok = P("expert", "dp")
    whole = P("expert", None)
    wide = P("expert", "dp", None)
    down = P("expert", None, "dp")
    return jax.shard_map(
        local,
        mesh=mesh,
        in_specs=(tok, whole, whole, wide, wide, down, tok),
        out_specs=(tok, tok, whole, wide, wide, down),
        check_vma=False,
    )
```

```python
import jax
import jax.numpy as jnp
from jax import lax
from jax.experimental import pallas as pl
from jax.experimental.pallas import tpu as pltpu
from jax.sharding import PartitionSpec as P

F32 = jnp.float32
BF16 = jnp.bfloat16
MESH = pl.DeviceIdType.MESH
NN = ((1,), (0,))
NT = ((1,), (1,))
TN = ((0,), (0,))


def dot(a, b, dims):
    return lax.dot_general(a, b, (dims, ((), ())), preferred_element_type=F32)


def kernel(
    rank_ref, weight_ref, tok_ref, og_ref, wg_hbm, wu_hbm, wd_hbm,
    mixed_ref, gtok_ref, route_ref, gg_hbm, gu_hbm, gd_hbm,
    wg, wu, wd, one, scaled, sent, xg, mine, held, far, act, back, st_g, st_u, st_d,
    acc_m, acc_t, dr_all, dr_in,
    w_sem, o_sem, d_send, d_recv, h_send, h_recv, r_send, r_recv, a_send, a_recv, c_send, c_recv,
    t_send, t_recv, q_send, q_recv, v_send, v_recv,
):
    n_e, _, rows, _ = sent.shape
    ff = wg.shape[2]
    n_o = lax.axis_size("expert")
    n_dp = lax.axis_size("dp")
    n_y = n_dp // 2
    cap = rows // n_o
    half = rows // 2
    part = half // n_y
    dp = lax.axis_index("dp")
    me = lax.axis_index("expert")
    y, core = dp // 2, dp % 2
    share = core * n_y + y
    own0 = pl.multiple_of(core * half, half)
    other0 = pl.multiple_of((1 - core) * half, half)
    part0 = pl.multiple_of(own0 + y * part, part)

    def remote(src, dst, ss, rs, d, o):
        return pltpu.make_async_remote_copy(
            src_ref=src, dst_ref=dst, send_sem=ss, recv_sem=rs, device_id=(d, o), device_id_type=MESH
        )

    def block(o):
        return pl.ds(pl.multiple_of(o * cap, cap), cap)

    def drain(ref, sem):
        pltpu.make_async_copy(ref, ref, sem).wait()

    loads = [pltpu.make_async_copy(h, v, w_sem.at[i]) for i, (h, v) in enumerate(((wg_hbm, wg), (wu_hbm, wu), (wd_hbm, wd)))]
    for c in loads:
        c.start()

    barrier = pltpu.get_barrier_semaphore()

    @pl.loop(1, n_o)
    def _(k):
        pl.semaphore_signal(barrier, inc=1, device_id=(dp, lax.rem(me + k, n_o)), device_id_type=MESH)

    @pl.loop(1, n_dp)
    def _(k):
        pl.semaphore_signal(barrier, inc=1, device_id=(lax.rem(dp + k, n_dp), me), device_id_type=MESH)

    def build(e):
        @pl.loop(0, n_o)
        def _(o):
            i = e * n_o + o
            r = rank_ref[pl.ds(i, 1), :]
            w = weight_ref[pl.ds(i, 1), :]
            m = r == lax.broadcasted_iota(jnp.int32, (cap, r.shape[1]), 0)
            at = pl.ds(pl.multiple_of(i * cap, cap), cap)
            one[at, :] = jnp.where(m, 1.0, 0.0).astype(BF16)
            scaled[at, :] = jnp.where(m, w, 0.0).astype(BF16)

        for half_, (mat, src) in enumerate(((one, tok_ref), (scaled, og_ref))):
            @pl.loop(0, rows // 256)
            def _(i, half_=half_, mat=mat, src=src):
                r0 = pl.multiple_of(i * 256, 256)
                sent[e, half_, pl.ds(r0, 256), :] = dot(mat[pl.ds(e * rows + r0, 256), :], src[...], NN).astype(BF16)

    def spread(src, dst, ss, rs, e):
        for h in range(2):
            @pl.loop(1, n_o)
            def _(k, h=h):
                to = lax.rem(me + k, n_o)
                remote(src.at[e, h, block(to)], dst.at[e, h, block(me)], ss.at[e, h], rs.at[e, h], dp, to).start()
            pltpu.make_async_copy(src.at[e, h, block(me)], dst.at[e, h, block(me)], rs.at[e, h]).start()

    def sent_all(e, ss):
        for h in range(2):
            drain(sent.at[e, h, pl.ds(0, rows - cap)], ss.at[e, h])

    def product(e, r0, store):
        @pl.loop(0, half // 192)
        def _(i):
            at = pl.ds(pl.multiple_of(r0 + i * 192, 192), 192)
            to = pl.ds(pl.multiple_of(i * 192, 192), 192)
            x = xg[e, 0, at, :]
            g = xg[e, 1, at, :]
            store[to, 0:ff] = dot(x, wg[e], NN).astype(BF16)
            store[to, ff : 2 * ff] = dot(x, wu[e], NN).astype(BF16)
            store[to, 2 * ff : 3 * ff] = dot(g, wd[e], NT).astype(BF16)

    def stage_d(e):
        for h in range(2):
            drain(xg.at[e, h], d_recv.at[e, h])
        if e == 0:
            for c in loads:
                c.wait()
        product(e, other0, mine.at[2])
        remote(mine.at[2], held.at[e % 2], h_send.at[e], h_recv.at[e], y * 2 + 1 - core, me).start()
        product(e, own0, mine.at[e % 2])

    left, right = lax.rem(y + n_y - 1, n_y), lax.rem(y + 1, n_y)
    across = lax.rem(y + 2, n_y)
    hp = part // 2

    def piece(y_, h):
        return pl.ds(pl.multiple_of(y_ * part + h * hp, hp), hp)

    def hop(e, i):
        to, y_, h, dst = (
            (left, across, 0, (2, 0)), (right, across, 1, (2, 1)),
            (left, left, 1, (0, 1)), (right, right, 0, (1, 0)),
            (left, left, 0, (0, 0)), (right, right, 1, (1, 1)),
        )[i]
        return remote(
            mine.at[e % 2, piece(y_, h)], far.at[e, dst[0], pl.ds(dst[1] * hp, hp)],
            r_send.at[e, i], r_recv.at[e, i], to * 2 + core, me,
        )

    def stage_r(e):
        cp = remote(mine.at[2], held.at[e % 2], h_send.at[e], h_recv.at[e], y * 2 + 1 - core, me)
        cp.wait_recv()
        for y_, go in ((across, (0, 1)), (left, (2,)), (right, (3,)), (y, ())):
            at = pl.ds(pl.multiple_of(y_ * part, part), part)
            own = mine.at[e % 2, at]
            own[...] = (own[...].astype(F32) + held[e % 2, at, :].astype(F32)).astype(BF16)
            for i in go:
                hop(e, i).start()
        cp.wait_send()

    def stage_p(e):
        for i, y_, h in ((0, left, 0), (1, right, 1)):
            hop(e, i).wait_recv()
            own = mine.at[e % 2, piece(y_, h)]
            own[...] = (own[...].astype(F32) + far[e, 2, h * hp : (h + 1) * hp, :].astype(F32)).astype(BF16)
            hop(e, i + 4).start()

    def relay(e, i):
        y_, r0, n, to = ((y, 0, part, right), (y, 0, part, left), (left, 0, hp, right), (right, hp, hp, left))[i]
        at = act.at[e % 3, pl.ds(pl.multiple_of(own0 + y_ * part + r0, hp), n)]
        return remote(at, at, a_send.at[e, i], a_recv.at[e, i], to * 2 + core, me)

    def stage_a(e):
        for i in range(2, 6):
            hop(e, i).wait_recv()
        at = pl.ds(pl.multiple_of(y * part, part), part)

        def total(c0):
            v = mine[e % 2, at, c0 : c0 + ff].astype(F32)
            for d in range(2):
                v = v + far[e, d, :, c0 : c0 + ff].astype(F32)
            return v

        gate, up, gh = total(0), total(ff), total(2 * ff)
        sig = 1.0 / (1.0 + jnp.exp(-gate))
        silu = gate * sig
        hid = (silu * up).astype(BF16)
        out = act.at[e % 3, pl.ds(part0, part)]
        out[:, 0:ff] = hid
        out[:, ff : 2 * ff] = (gh * up * sig * (1.0 + gate * (1.0 - sig))).astype(BF16)
        out[:, 2 * ff : 3 * ff] = (gh * silu).astype(BF16)
        relay(e, 0).start()
        relay(e, 1).start()
        prod = (hid.astype(F32) * gh).astype(BF16)
        row = dot(jnp.ones((8, ff), BF16), prod, NT)
        dr_all[share, e : e + 1, 0:part] = row[0:1]
        for i in range(6):
            hop(e, i).wait_send()

    def stage_g(e):
        for i in range(2):
            relay(e, i).wait_recv()
            relay(e, i + 2).start()

    def stage_f(e):
        for i in (2, 3):
            relay(e, i).wait_recv()
        for i in range(4):
            relay(e, i).wait_send()
        mine_ = act.at[e % 3, pl.ds(own0, half)]
        remote(mine_, mine_, c_send.at[e], c_recv.at[e], y * 2 + 1 - core, me).start()

    def stage_c(e):
        mine_ = act.at[e % 3, pl.ds(own0, half)]
        remote(mine_, mine_, c_send.at[e], c_recv.at[e], y * 2 + 1 - core, me).wait()
        sent_all(e, d_send)

        @pl.loop(0, rows // 256)
        def _(i):
            at = pl.ds(pl.multiple_of(i * 256, 256), 256)
            sent[e, 0, at, :] = dot(act[e % 3, at, 0:ff], wd[e], NN).astype(BF16)
            so = dot(act[e % 3, at, ff : 2 * ff], wg[e], NT) + dot(act[e % 3, at, 2 * ff : 3 * ff], wu[e], NT)
            sent[e, 1, at, :] = so.astype(BF16)

        spread(sent, back, t_send, t_recv, e)

    def stage_w(e):
        if e:
            for c in stored(e - 1):
                c.wait()

        @pl.loop(0, ff // 256)
        def _(i):
            at = pl.ds(pl.multiple_of(i * 256, 256), 256)
            st_d[at, :] = dot(act[e % 3, :, at], xg[e, 1], TN).astype(BF16)

        @pl.loop(0, xg.shape[3] // 256)
        def _(i):
            at = pl.ds(pl.multiple_of(i * 256, 256), 256)
            x = xg[e, 0, :, at]
            st_g[at, :] = dot(x, act[e % 3, :, ff : 2 * ff], TN).astype(BF16)
            st_u[at, :] = dot(x, act[e % 3, :, 2 * ff : 3 * ff], TN).astype(BF16)

        for c in stored(e):
            c.start()

    def stored(e):
        return (
            pltpu.make_async_copy(st_g, gg_hbm.at[e], o_sem.at[0]),
            pltpu.make_async_copy(st_u, gu_hbm.at[e], o_sem.at[1]),
            pltpu.make_async_copy(st_d, gd_hbm.at[e], o_sem.at[2]),
        )

    def gather(e):
        at = pl.ds(e * rows, rows)
        for h, (mat, acc) in enumerate(((scaled, acc_m), (one, acc_t))):
            drain(back.at[e, h], t_recv.at[e, h])
            v = dot(mat[at, :], back[e, h], TN)
            if e == 0:
                acc[...] = v
            else:
                acc[...] += v

    dr_all[share] = jnp.zeros(dr_all.shape[1:], F32)
    build(0)
    pl.semaphore_wait(barrier, n_o + n_dp - 2)
    spread(sent, xg, d_send, d_recv, 0)
    for e in range(1, n_e):
        build(e)
        spread(sent, xg, d_send, d_recv, e)
    for e in range(n_e):
        stage_d(e)
        stage_r(e)
        if e == 0:
            stage_p(0)
            stage_a(0)
            continue
        if e > 1:
            stage_w(e - 2)
        stage_g(e - 1)
        stage_p(e)
        stage_f(e - 1)
        stage_c(e - 1)
        stage_a(e)

    @pl.loop(1, n_dp)
    def _(k):
        own = dr_all.at[share]
        remote(own, own, q_send, q_recv, lax.rem(dp + k, n_dp), me).start()

    stage_g(3)
    stage_w(2)
    stage_f(3)
    drain(dr_all.at[pl.ds(0, n_dp - 1)], q_recv)
    drain(dr_all.at[pl.ds(0, n_dp - 1)], q_send)

    @pl.loop(1, n_o)
    def _(k):
        to = lax.rem(me + k, n_o)
        remote(dr_all.at[to // 2], dr_in.at[me], v_send, v_recv, dp, to).start()

    pltpu.make_async_copy(dr_all.at[me // 2], dr_in.at[me], v_recv).start()
    stage_c(3)
    stage_w(3)
    gather(0)
    gather(1)
    gather(2)
    drain(dr_in, v_recv)
    drain(dr_in.at[pl.ds(0, n_o - 1)], v_send)
    route_ref[...] = dr_in[...]
    gather(3)
    mixed_ref[...] = acc_m[...].astype(BF16)
    gtok_ref[...] = acc_t[...].astype(BF16)
    for e in range(n_e):
        sent_all(e, t_send)
    for c in stored(n_e - 1):
        c.wait()


def pass_on(*refs):
    n = (len(refs) - 2) // 3
    sems_in, sems_out = refs[-2:]
    arrive, leave = [], []
    for i, (a, b, v) in enumerate(zip(refs[:n], refs[n : 2 * n], refs[2 * n : 3 * n])):
        for p in range(a.shape[0]):
            arrive.append(pltpu.make_async_copy(a.at[p], v.at[p], sems_in.at[i, p]))
            leave.append(pltpu.make_async_copy(v.at[p], b.at[p], sems_out.at[i, p]))
    for c in arrive:
        c.start()
    for c, d in zip(arrive, leave):
        c.wait()
        d.start()
    for d in leave:
        d.wait()


def local(tokens, expert_ids, route_weights, w_gate, w_up, w_down, out_grad):
    tok, top = expert_ids.shape
    e_loc, width, ff = w_gate.shape
    owners = lax.axis_size("expert")
    n_dp = lax.axis_size("dp")
    experts = e_loc * owners
    cap = 3 * tok * top // (2 * experts)
    rows = owners * cap
    half, part = rows // 2, rows // n_dp
    table = jnp.arange(experts, dtype=jnp.int32)
    hit = expert_ids[:, :, None] == table
    member = jnp.any(hit, 1)
    tri = (jnp.arange(tok)[:, None] > jnp.arange(tok)[None, :]).astype(BF16)
    before = jnp.dot(tri, member.astype(BF16), preferred_element_type=F32).astype(jnp.int32)
    rank = jnp.where(member, before, -1)
    rounded = route_weights.astype(BF16).astype(F32)
    weight = jnp.sum(jnp.where(hit, rounded[:, :, None], 0.0), 1)

    def order(v):
        return v.T.reshape(owners, e_loc, tok).transpose(1, 0, 2).reshape(experts, tok)

    rank, weight = order(rank), order(weight)
    vm = pl.BlockSpec(memory_space=pltpu.VMEM)
    hbm = pl.BlockSpec(memory_space=pl.ANY)
    dma = pltpu.SemaphoreType.DMA
    mixed, gtok, route, gg, gu, gd = pl.pallas_call(
        kernel,
        out_shape=(
            jax.ShapeDtypeStruct((tok, width), BF16),
            jax.ShapeDtypeStruct((tok, width), BF16),
            jax.ShapeDtypeStruct((owners, 8, 128), F32),
            jax.ShapeDtypeStruct((e_loc, width, ff), BF16),
            jax.ShapeDtypeStruct((e_loc, width, ff), BF16),
            jax.ShapeDtypeStruct((e_loc, ff, width), BF16),
        ),
        in_specs=[vm] * 4 + [hbm] * 3,
        out_specs=[vm] * 3 + [hbm] * 3,
        scratch_shapes=[
            pltpu.VMEM((e_loc, width, ff), BF16),
            pltpu.VMEM((e_loc, width, ff), BF16),
            pltpu.VMEM((e_loc, ff, width), BF16),
            pltpu.VMEM((e_loc * rows, tok), BF16),
            pltpu.VMEM((e_loc * rows, tok), BF16),
            pltpu.VMEM((e_loc, 2, rows, width), BF16),
            pltpu.VMEM((e_loc, 2, rows, width), BF16),
            pltpu.VMEM((3, half, 3 * ff), BF16),
            pltpu.VMEM((2, half, 3 * ff), BF16),
            pltpu.VMEM((e_loc, 3, part, 3 * ff), BF16),
            pltpu.VMEM((3, rows, 3 * ff), BF16),
            pltpu.VMEM((e_loc, 2, rows, width), BF16),
            pltpu.VMEM((width, ff), BF16),
            pltpu.VMEM((width, ff), BF16),
            pltpu.VMEM((ff, width), BF16),
            pltpu.VMEM((tok, width), F32),
            pltpu.VMEM((tok, width), F32),
            pltpu.VMEM((n_dp, 8, 128), F32),
            pltpu.VMEM((owners, 8, 128), F32),
            dma((3,)), dma((3,)), dma((4, 2)), dma((4, 2)), dma((4,)), dma((4,)),
            dma((4, 6)), dma((4, 6)), dma((4, 4)), dma((4, 4)), dma((4,)), dma((4,)),
            dma((4, 2)), dma((4, 2)), dma, dma, dma, dma,
        ],
        compiler_params=pltpu.CompilerParams(
            collective_id=0, has_side_effects=True, vmem_limit_bytes=61 * 2**20
        ),
        name="moe",
    )(rank, weight, tokens, out_grad, w_gate, w_up, w_down)
    results = (gg, gu, gd)
    gg, gu, gd = pl.pallas_call(
        pass_on,
        out_shape=tuple(jax.ShapeDtypeStruct(v.shape, v.dtype) for v in results),
        in_specs=[hbm] * 3,
        out_specs=[hbm] * 3,
        scratch_shapes=[pltpu.VMEM(v.shape, v.dtype) for v in results] + [dma((3, e_loc)), dma((3, e_loc))],
        compiler_params=pltpu.CompilerParams(vmem_limit_bytes=60 * 2**20),
        name="pass_on",
    )(*results)
    at = (lax.axis_index("expert") % 2) * cap
    per = lax.dynamic_slice_in_dim(route[:, :e_loc], at, cap, 2)
    per = per.transpose(1, 0, 2).reshape(experts, cap)
    pick = rank[:, None, :] == jnp.arange(cap, dtype=jnp.int32)[None, :, None]
    value = jnp.sum(jnp.where(pick, per[:, :, None], 0.0), 1)
    value = value.reshape(e_loc, owners, tok).transpose(1, 0, 2).reshape(experts, tok)
    grad_route = jnp.sum(jnp.where(hit, value.T[:, None, :], 0.0), 2) / rounded
    return (mixed, gtok, grad_route, gg, gu, gd)


def solution(mesh):
    tok = P("expert", "dp")
    whole = P("expert", None)
    wide = P("expert", "dp", None)
    down = P("expert", None, "dp")
    return jax.shard_map(
        local,
        mesh=mesh,
        in_specs=(tok, whole, whole, wide, wide, down, tok),
        out_specs=(tok, tok, whole, wide, wide, down),
        check_vma=False,
    )
```

```python
import jax
import jax.numpy as jnp
from jax import lax
from jax.experimental import pallas as pl
from jax.experimental.pallas import tpu as pltpu
from jax.sharding import PartitionSpec as P

F32 = jnp.float32
BF16 = jnp.bfloat16
MESH = pl.DeviceIdType.MESH
NN = ((1,), (0,))
NT = ((1,), (1,))
TN = ((0,), (0,))


def dot(a, b, dims):
    return lax.dot_general(a, b, (dims, ((), ())), preferred_element_type=F32)


def kernel(
    rank_ref, weight_ref, tok_ref, og_ref, wg_hbm, wu_hbm, wd_hbm,
    mixed_ref, gtok_ref, route_ref, gg_hbm, gu_hbm, gd_hbm,
    wg, wu, wd, one, scaled, sent, xg, mine, held, far, act, back, st_g, st_u, st_d,
    acc_m, acc_t, dr_all, dr_in,
    w_sem, o_sem, d_send, d_recv, h_send, h_recv, r_send, r_recv, a_send, a_recv, c_send, c_recv,
    t_send, t_recv, q_send, q_recv, v_send, v_recv,
):
    n_e, _, rows, _ = sent.shape
    ff = wg.shape[2]
    n_o = lax.axis_size("expert")
    n_dp = lax.axis_size("dp")
    n_y = n_dp // 2
    cap = rows // n_o
    half = rows // 2
    part = half // n_y
    dp = lax.axis_index("dp")
    me = lax.axis_index("expert")
    y, core = dp // 2, dp % 2
    share = core * n_y + y
    own0 = pl.multiple_of(core * half, half)
    other0 = pl.multiple_of((1 - core) * half, half)
    part0 = pl.multiple_of(own0 + y * part, part)

    def remote(src, dst, ss, rs, d, o):
        return pltpu.make_async_remote_copy(
            src_ref=src, dst_ref=dst, send_sem=ss, recv_sem=rs, device_id=(d, o), device_id_type=MESH
        )

    def block(o):
        return pl.ds(pl.multiple_of(o * cap, cap), cap)

    def drain(ref, sem):
        pltpu.make_async_copy(ref, ref, sem).wait()

    loads = [pltpu.make_async_copy(h, v, w_sem.at[i]) for i, (h, v) in enumerate(((wg_hbm, wg), (wu_hbm, wu), (wd_hbm, wd)))]
    for c in loads:
        c.start()

    barrier = pltpu.get_barrier_semaphore()

    @pl.loop(1, n_o)
    def _(k):
        pl.semaphore_signal(barrier, inc=1, device_id=(dp, lax.rem(me + k, n_o)), device_id_type=MESH)

    @pl.loop(1, n_dp)
    def _(k):
        pl.semaphore_signal(barrier, inc=1, device_id=(lax.rem(dp + k, n_dp), me), device_id_type=MESH)

    def build(e):
        @pl.loop(0, n_o)
        def _(o):
            i = e * n_o + o
            r = rank_ref[pl.ds(i, 1), :]
            w = weight_ref[pl.ds(i, 1), :]
            m = r == lax.broadcasted_iota(jnp.int32, (cap, r.shape[1]), 0)
            at = pl.ds(pl.multiple_of(i * cap, cap), cap)
            one[at, :] = jnp.where(m, 1.0, 0.0).astype(BF16)
            scaled[at, :] = jnp.where(m, w, 0.0).astype(BF16)

        for half_, (mat, src) in enumerate(((one, tok_ref), (scaled, og_ref))):
            @pl.loop(0, rows // 256)
            def _(i, half_=half_, mat=mat, src=src):
                r0 = pl.multiple_of(i * 256, 256)
                sent[e, half_, pl.ds(r0, 256), :] = dot(mat[pl.ds(e * rows + r0, 256), :], src[...], NN).astype(BF16)

    ex, ez = me // 4, me % 4
    peers = [lax.rem(ex + dx, 4) * 4 + lax.rem(ez + dz, 4) for dx, dz in ((2, 2), (0, 1), (2, 1), (3, 0), (1, 2), (0, 3), (2, 3), (1, 0), (3, 2), (1, 1), (2, 0), (3, 3), (0, 2), (1, 3), (3, 1))]

    def spread(src, dst, ss, rs, e, hs=(0, 1)):
        for h in hs:
            for to in peers:
                remote(src.at[e, h, block(to)], dst.at[e, h, block(me)], ss.at[e, h], rs.at[e, h], dp, to).start()
            pltpu.make_async_copy(src.at[e, h, block(me)], dst.at[e, h, block(me)], rs.at[e, h]).start()

    def sent_all(e, ss):
        for h in range(2):
            drain(sent.at[e, h, pl.ds(0, rows - cap)], ss.at[e, h])

    def product(e, r0, store):
        @pl.loop(0, half // 192)
        def _(i):
            at = pl.ds(pl.multiple_of(r0 + i * 192, 192), 192)
            to = pl.ds(pl.multiple_of(i * 192, 192), 192)
            x = xg[e, 0, at, :]
            g = xg[e, 1, at, :]
            store[to, 0:ff] = dot(x, wg[e], NN).astype(BF16)
            store[to, ff : 2 * ff] = dot(x, wu[e], NN).astype(BF16)
            store[to, 2 * ff : 3 * ff] = dot(g, wd[e], NT).astype(BF16)

    def stage_d(e):
        for h in range(2):
            drain(xg.at[e, h], d_recv.at[e, h])
        if e == 0:
            for c in loads:
                c.wait()
        product(e, other0, mine.at[2])
        remote(mine.at[2], held.at[e % 2], h_send.at[e], h_recv.at[e], y * 2 + 1 - core, me).start()
        product(e, own0, mine.at[e % 2])

    left, right = lax.rem(y + n_y - 1, n_y), lax.rem(y + 1, n_y)
    across = lax.rem(y + 2, n_y)
    hp = part // 2

    def piece(y_, h):
        return pl.ds(pl.multiple_of(y_ * part + h * hp, hp), hp)

    def hop(e, i):
        to, y_, h, dst = (
            (left, across, 0, (2, 0)), (right, across, 1, (2, 1)),
            (left, left, 1, (0, 1)), (right, right, 0, (1, 0)),
            (left, left, 0, (0, 0)), (right, right, 1, (1, 1)),
        )[i]
        return remote(
            mine.at[e % 2, piece(y_, h)], far.at[e, dst[0], pl.ds(dst[1] * hp, hp)],
            r_send.at[e, i], r_recv.at[e, i], to * 2 + core, me,
        )

    def stage_r(e):
        cp = remote(mine.at[2], held.at[e % 2], h_send.at[e], h_recv.at[e], y * 2 + 1 - core, me)
        cp.wait_recv()
        for y_, go in ((across, (0, 1)), (left, (2,)), (right, (3,)), (y, ())):
            at = pl.ds(pl.multiple_of(y_ * part, part), part)
            own = mine.at[e % 2, at]
            own[...] = (own[...].astype(F32) + held[e % 2, at, :].astype(F32)).astype(BF16)
            for i in go:
                hop(e, i).start()
        cp.wait_send()

    def stage_p(e):
        for i, y_, h in ((0, left, 0), (1, right, 1)):
            hop(e, i).wait_recv()
            own = mine.at[e % 2, piece(y_, h)]
            own[...] = (own[...].astype(F32) + far[e, 2, h * hp : (h + 1) * hp, :].astype(F32)).astype(BF16)
            hop(e, i + 4).start()

    def relay(e, i):
        y_, r0, n, to = ((y, 0, part, right), (y, 0, part, left), (left, 0, hp, right), (right, hp, hp, left))[i]
        at = act.at[e % 3, pl.ds(pl.multiple_of(own0 + y_ * part + r0, hp), n)]
        return remote(at, at, a_send.at[e, i], a_recv.at[e, i], to * 2 + core, me)

    def stage_a(e):
        for i in range(2, 6):
            hop(e, i).wait_recv()
        at = pl.ds(pl.multiple_of(y * part, part), part)

        def total(c0):
            v = mine[e % 2, at, c0 : c0 + ff].astype(F32)
            for d in range(2):
                v = v + far[e, d, :, c0 : c0 + ff].astype(F32)
            return v

        gate, up, gh = total(0), total(ff), total(2 * ff)
        sig = 1.0 / (1.0 + jnp.exp(-gate))
        silu = gate * sig
        hid = (silu * up).astype(BF16)
        out = act.at[e % 3, pl.ds(part0, part)]
        out[:, 0:ff] = hid
        out[:, ff : 2 * ff] = (gh * up * sig * (1.0 + gate * (1.0 - sig))).astype(BF16)
        out[:, 2 * ff : 3 * ff] = (gh * silu).astype(BF16)
        relay(e, 0).start()
        relay(e, 1).start()
        prod = (hid.astype(F32) * gh).astype(BF16)
        row = dot(jnp.ones((8, ff), BF16), prod, NT)
        dr_all[share, e : e + 1, 0:part] = row[0:1]
        for i in range(6):
            hop(e, i).wait_send()

    def stage_g(e):
        for i in range(2):
            relay(e, i).wait_recv()
            relay(e, i + 2).start()

    def stage_f(e):
        for i in (2, 3):
            relay(e, i).wait_recv()
        for i in range(4):
            relay(e, i).wait_send()
        mine_ = act.at[e % 3, pl.ds(own0, half)]
        remote(mine_, mine_, c_send.at[e], c_recv.at[e], y * 2 + 1 - core, me).start()

    def stage_c(e):
        mine_ = act.at[e % 3, pl.ds(own0, half)]
        remote(mine_, mine_, c_send.at[e], c_recv.at[e], y * 2 + 1 - core, me).wait()
        sent_all(e, d_send)

        @pl.loop(0, rows // 256)
        def _(i):
            at = pl.ds(pl.multiple_of(i * 256, 256), 256)
            sent[e, 0, at, :] = dot(act[e % 3, at, 0:ff], wd[e], NN).astype(BF16)

        spread(sent, back, t_send, t_recv, e, (0,))

        @pl.loop(0, rows // 256)
        def _(i):
            at = pl.ds(pl.multiple_of(i * 256, 256), 256)
            so = dot(act[e % 3, at, ff : 2 * ff], wg[e], NT) + dot(act[e % 3, at, 2 * ff : 3 * ff], wu[e], NT)
            sent[e, 1, at, :] = so.astype(BF16)

        spread(sent, back, t_send, t_recv, e, (1,))

    def stage_w(e):
        if e:
            for c in stored(e - 1):
                c.wait()

        @pl.loop(0, ff // 256)
        def _(i):
            at = pl.ds(pl.multiple_of(i * 256, 256), 256)
            st_d[at, :] = dot(act[e % 3, :, at], xg[e, 1], TN).astype(BF16)

        @pl.loop(0, xg.shape[3] // 256)
        def _(i):
            at = pl.ds(pl.multiple_of(i * 256, 256), 256)
            x = xg[e, 0, :, at]
            st_g[at, :] = dot(x, act[e % 3, :, ff : 2 * ff], TN).astype(BF16)
            st_u[at, :] = dot(x, act[e % 3, :, 2 * ff : 3 * ff], TN).astype(BF16)

        for c in stored(e):
            c.start()

    def stored(e):
        return (
            pltpu.make_async_copy(st_g, gg_hbm.at[e], o_sem.at[0]),
            pltpu.make_async_copy(st_u, gu_hbm.at[e], o_sem.at[1]),
            pltpu.make_async_copy(st_d, gd_hbm.at[e], o_sem.at[2]),
        )

    def gather(e):
        at = pl.ds(e * rows, rows)
        for h, (mat, acc) in enumerate(((scaled, acc_m), (one, acc_t))):
            drain(back.at[e, h], t_recv.at[e, h])
            v = dot(mat[at, :], back[e, h], TN)
            if e == 0:
                acc[...] = v
            else:
                acc[...] += v

    dr_all[share] = jnp.zeros(dr_all.shape[1:], F32)
    build(0)
    pl.semaphore_wait(barrier, n_o + n_dp - 2)
    spread(sent, xg, d_send, d_recv, 0)
    build(1)
    spread(sent, xg, d_send, d_recv, 1)
    build(2)
    build(3)
    for e in range(n_e):
        stage_d(e)
        if e + 2 < n_e:
            spread(sent, xg, d_send, d_recv, e + 2)
        stage_r(e)
        if e == 0:
            stage_p(0)
            stage_a(0)
            continue
        if e > 1:
            stage_w(e - 2)
        stage_g(e - 1)
        stage_p(e)
        stage_f(e - 1)
        stage_c(e - 1)
        stage_a(e)

    @pl.loop(1, n_dp)
    def _(k):
        own = dr_all.at[share]
        remote(own, own, q_send, q_recv, lax.rem(dp + k, n_dp), me).start()

    stage_g(3)
    stage_w(2)
    stage_f(3)
    drain(dr_all.at[pl.ds(0, n_dp - 1)], q_recv)
    drain(dr_all.at[pl.ds(0, n_dp - 1)], q_send)

    @pl.loop(1, n_o)
    def _(k):
        to = lax.rem(me + k, n_o)
        remote(dr_all.at[to // 2], dr_in.at[me], v_send, v_recv, dp, to).start()

    pltpu.make_async_copy(dr_all.at[me // 2], dr_in.at[me], v_recv).start()
    stage_c(3)
    stage_w(3)
    gather(0)
    gather(1)
    gather(2)
    drain(dr_in, v_recv)
    drain(dr_in.at[pl.ds(0, n_o - 1)], v_send)
    route_ref[...] = dr_in[...]
    gather(3)
    mixed_ref[...] = acc_m[...].astype(BF16)
    gtok_ref[...] = acc_t[...].astype(BF16)
    for e in range(n_e):
        sent_all(e, t_send)
    for c in stored(n_e - 1):
        c.wait()


def pass_on(*refs):
    n = (len(refs) - 2) // 3
    sems_in, sems_out = refs[-2:]
    arrive, leave = [], []
    for i, (a, b, v) in enumerate(zip(refs[:n], refs[n : 2 * n], refs[2 * n : 3 * n])):
        for p in range(a.shape[0]):
            arrive.append(pltpu.make_async_copy(a.at[p], v.at[p], sems_in.at[i, p]))
            leave.append(pltpu.make_async_copy(v.at[p], b.at[p], sems_out.at[i, p]))
    for c in arrive:
        c.start()
    for c, d in zip(arrive, leave):
        c.wait()
        d.start()
    for d in leave:
        d.wait()


def local(tokens, expert_ids, route_weights, w_gate, w_up, w_down, out_grad):
    tok, top = expert_ids.shape
    e_loc, width, ff = w_gate.shape
    owners = lax.axis_size("expert")
    n_dp = lax.axis_size("dp")
    experts = e_loc * owners
    cap = 3 * tok * top // (2 * experts)
    rows = owners * cap
    half, part = rows // 2, rows // n_dp
    table = jnp.arange(experts, dtype=jnp.int32)
    hit = expert_ids[:, :, None] == table
    member = jnp.any(hit, 1)
    tri = (jnp.arange(tok)[:, None] > jnp.arange(tok)[None, :]).astype(BF16)
    before = jnp.dot(tri, member.astype(BF16), preferred_element_type=F32).astype(jnp.int32)
    rank = jnp.where(member, before, -1)
    rounded = route_weights.astype(BF16).astype(F32)
    weight = jnp.sum(jnp.where(hit, rounded[:, :, None], 0.0), 1)

    def order(v):
        return v.T.reshape(owners, e_loc, tok).transpose(1, 0, 2).reshape(experts, tok)

    rank, weight = order(rank), order(weight)
    vm = pl.BlockSpec(memory_space=pltpu.VMEM)
    hbm = pl.BlockSpec(memory_space=pl.ANY)
    dma = pltpu.SemaphoreType.DMA
    mixed, gtok, route, gg, gu, gd = pl.pallas_call(
        kernel,
        out_shape=(
            jax.ShapeDtypeStruct((tok, width), BF16),
            jax.ShapeDtypeStruct((tok, width), BF16),
            jax.ShapeDtypeStruct((owners, 8, 128), F32),
            jax.ShapeDtypeStruct((e_loc, width, ff), BF16),
            jax.ShapeDtypeStruct((e_loc, width, ff), BF16),
            jax.ShapeDtypeStruct((e_loc, ff, width), BF16),
        ),
        in_specs=[vm] * 4 + [hbm] * 3,
        out_specs=[vm] * 3 + [hbm] * 3,
        scratch_shapes=[
            pltpu.VMEM((e_loc, width, ff), BF16),
            pltpu.VMEM((e_loc, width, ff), BF16),
            pltpu.VMEM((e_loc, ff, width), BF16),
            pltpu.VMEM((e_loc * rows, tok), BF16),
            pltpu.VMEM((e_loc * rows, tok), BF16),
            pltpu.VMEM((e_loc, 2, rows, width), BF16),
            pltpu.VMEM((e_loc, 2, rows, width), BF16),
            pltpu.VMEM((3, half, 3 * ff), BF16),
            pltpu.VMEM((2, half, 3 * ff), BF16),
            pltpu.VMEM((e_loc, 3, part, 3 * ff), BF16),
            pltpu.VMEM((3, rows, 3 * ff), BF16),
            pltpu.VMEM((e_loc, 2, rows, width), BF16),
            pltpu.VMEM((width, ff), BF16),
            pltpu.VMEM((width, ff), BF16),
            pltpu.VMEM((ff, width), BF16),
            pltpu.VMEM((tok, width), F32),
            pltpu.VMEM((tok, width), F32),
            pltpu.VMEM((n_dp, 8, 128), F32),
            pltpu.VMEM((owners, 8, 128), F32),
            dma((3,)), dma((3,)), dma((4, 2)), dma((4, 2)), dma((4,)), dma((4,)),
            dma((4, 6)), dma((4, 6)), dma((4, 4)), dma((4, 4)), dma((4,)), dma((4,)),
            dma((4, 2)), dma((4, 2)), dma, dma, dma, dma,
        ],
        compiler_params=pltpu.CompilerParams(
            collective_id=0, has_side_effects=True, vmem_limit_bytes=61 * 2**20
        ),
        name="moe",
    )(rank, weight, tokens, out_grad, w_gate, w_up, w_down)
    results = (gg, gu, gd)
    gg, gu, gd = pl.pallas_call(
        pass_on,
        out_shape=tuple(jax.ShapeDtypeStruct(v.shape, v.dtype) for v in results),
        in_specs=[hbm] * 3,
        out_specs=[hbm] * 3,
        scratch_shapes=[pltpu.VMEM(v.shape, v.dtype) for v in results] + [dma((3, e_loc)), dma((3, e_loc))],
        compiler_params=pltpu.CompilerParams(vmem_limit_bytes=60 * 2**20),
        name="pass_on",
    )(*results)
    at = (lax.axis_index("expert") % 2) * cap
    per = lax.dynamic_slice_in_dim(route[:, :e_loc], at, cap, 2)
    per = per.transpose(1, 0, 2).reshape(experts, cap)
    pick = rank[:, None, :] == jnp.arange(cap, dtype=jnp.int32)[None, :, None]
    value = jnp.sum(jnp.where(pick, per[:, :, None], 0.0), 1)
    value = value.reshape(e_loc, owners, tok).transpose(1, 0, 2).reshape(experts, tok)
    grad_route = jnp.sum(jnp.where(hit, value.T[:, None, :], 0.0), 2) / rounded
    return (mixed, gtok, grad_route, gg, gu, gd)


def solution(mesh):
    tok = P("expert", "dp")
    whole = P("expert", None)
    wide = P("expert", "dp", None)
    down = P("expert", None, "dp")
    return jax.shard_map(
        local,
        mesh=mesh,
        in_specs=(tok, whole, whole, wide, wide, down, tok),
        out_specs=(tok, tok, whole, wide, wide, down),
        check_vma=False,
    )
```
